32 devices in a mesh: section: 2 (over core), dp: 16 (over z, y, x).
Axes of the slice: x: 2, y: 2, z: 4, core: 2. Of those that a mesh axis runs over, the one named last changes fastest.
Arguments:
- tokens: bfloat16 [2, 8192, 768], P(None, 'dp'), may hold values from -6 to 6
- lengths: int32 [2, 16, 4], P(None, 'dp'), may hold values from 1 to 320, 512 in all within a row
- cotangent: bfloat16 [2, 8192, 768], P(None, 'dp'), may hold values from -6 to 6
- qkv_weight: bfloat16 [2, 768, 2304], P('section', 'dp'), may hold values from -0.21875 to 0.21875
- out_weight: bfloat16 [2, 768, 768], P('section', 'dp'), may hold values from -0.875 to 0.875
- up_weight: bfloat16 [2, 768, 3072], P('section', 'dp'), may hold values from -0.21875 to 0.21875
- down_weight: bfloat16 [2, 3072, 768], P('section', 'dp'), may hold values from -0.109375 to 0.109375
- qkv_bias: bfloat16 [2, 2304], P('section', 'dp'), may hold values from -1.5 to 1.5
- out_bias: bfloat16 [2, 768], P('section', 'dp'), may hold values from -1.5 to 1.5
- up_bias: bfloat16 [2, 3072], P('section', 'dp'), may hold values from -1.5 to 1.5
- down_bias: bfloat16 [2, 768], P('section', 'dp'), may hold values from -1.5 to 1.5
- attn_gain: bfloat16 [2, 768], P('section', 'dp'), may hold values from 0.5 to 1.5
- attn_shift: bfloat16 [2, 768], P('section', 'dp'), may hold values from -1.5 to 1.5
- mlp_gain: bfloat16 [2, 768], P('section', 'dp'), may hold values from 0.5 to 1.5
- mlp_shift: bfloat16 [2, 768], P('section', 'dp'), may hold values from -1.5 to 1.5
Outputs:
- layer_outputs: bfloat16 [2, 2, 8192, 768], P('section', None, 'dp')
- input_grads: float32 [2, 2, 8192, 768], P('section', None, 'dp')
- grad_qkv_weight: float32 [2, 768, 2304], P('section', 'dp')
- grad_out_weight: float32 [2, 768, 768], P('section', 'dp')
- grad_up_weight: float32 [2, 768, 3072], P('section', 'dp')
- grad_down_weight: float32 [2, 3072, 768], P('section', 'dp')
- grad_qkv_bias: float32 [2, 2304], P('section', 'dp')
- grad_out_bias: float32 [2, 768], P('section', 'dp')
- grad_up_bias: float32 [2, 3072], P('section', 'dp')
- grad_down_bias: float32 [2, 768], P('section', 'dp')
- grad_attn_gain: float32 [2, 768], P('section', 'dp')
- grad_attn_shift: float32 [2, 768], P('section', 'dp')
- grad_mlp_gain: float32 [2, 768], P('section', 'dp')
- grad_mlp_shift: float32 [2, 768], P('section', 'dp')
The draws below stay inside these ranges and needn't reach their ends.
Inputs may be any that keep to these rules, and one draw needn't show every extreme that they name: Each row lengths[m, j, :] sums to 512, and its longest sequence has exactly 320 tokens.
All inputs are finite; a program needn't handle non-finite values.
Results may differ from the reference program's by a relative error of at most 0.012.
Values may be sent and summed in bfloat16 or wider, within the bound.
A program may use at most 256 MiB of HBM per device.

```python
import math
import jax
import jax.numpy as jnp
import numpy as np
from jax import lax

D = 768
FF = 3072
TOK_MB = 512
MB = 2
SEQS = 4
SEQ_MOST = 320
TOKENS = 8192
N_DP = 16


def strengthened(array, rng, source, target, parts, factor):
    owner, partner = [(jnp.arange(array.shape[dim]) // (array.shape[dim] // parts)).reshape([-1 if axis == dim else 1 for axis in range(array.ndim)]) for dim in (source, target)]
    chosen = jax.random.permutation(rng, parts)[partner]
    strong = (owner == chosen) | (owner == (partner + parts // 2) % parts)
    return jnp.where(strong, factor * array, array)


def block_scale(key, extent, pieces, low, largest):
    def one(axis_at, shards_of):
        heights = jax.random.uniform(jax.random.fold_in(jax.random.fold_in(key, 6), axis_at), (shards_of,), jnp.float32, low / len(pieces), largest / len(pieces))
        return jnp.repeat(jnp.exp(heights), extent[axis_at] // shards_of).reshape((-1,) + (1,) * (len(extent) - axis_at - 1))

    level = one(*pieces[0])
    for cut in pieces[1:]:
        level = level * one(*cut)
    return level


def split_up(amount, total, limit, skew):
    portions = [(1 << 20) // math.isqrt(grade ** skew) + 1 for grade in range(2, amount + 1)]
    surplus, counts = total - limit - (amount - 1), [1] * (amount - 1)
    while surplus > 0:
        candidates = [i for i in range(amount - 1) if counts[i] < limit]
        mass, remaining = sum([portions[i] for i in candidates]), surplus
        for i in candidates:
            extra = min(limit - counts[i], max(1, remaining * portions[i] // mass), surplus)
            counts[i] = counts[i] + extra
            surplus = surplus - extra
    return np.array([limit] + counts)


def uneven_parts(own_key, count, total, most, slope):
    if count == 2:
        one = jax.random.randint(own_key, (), max(1, total - most), min(most, total - 1) + 1)
        return jnp.stack([one, total - one])
    sizes = jnp.asarray(split_up(count, total, most, slope), jnp.int32)
    twos = (count - 1) // 2
    source_of, receiver = sizes[1:1 + 2 * twos:2], sizes[2:2 + 2 * twos:2]
    margin = jnp.minimum(source_of - 1, most - receiver)
    shifted = jax.random.randint(jax.random.fold_in(own_key, 1), (twos,), 0, 1 << 20) % (margin + 1)
    sizes = sizes.at[1:1 + 2 * twos:2].set(source_of - shifted).at[2:2 + 2 * twos:2].set(receiver + shifted)
    return sizes[jax.random.permutation(jax.random.fold_in(own_key, 2), count)]


def normal_values(own_key, dims, scale, reach, pieces=(), kind=jnp.bfloat16):
    values = jax.random.normal(own_key, dims, jnp.float32) * scale
    if len(pieces) > 0:
        values = block_scale(own_key, dims, pieces, -0.22, 0.18) * values
    return jnp.clip(values, min=-reach, max=reach).astype(kind)


def bell_draw_with(stream_key, dims, scale, limit, cuts, heavy, kind=jnp.bfloat16):
    drawn = scale * jax.random.normal(stream_key, dims, jnp.float32)
    if cuts:
        drawn = drawn * block_scale(stream_key, dims, cuts, -0.22, 0.18)
    return jnp.clip(strengthened(drawn, jax.random.fold_in(stream_key, 3), *heavy), -limit, limit).astype(kind)


def setup_inputs(seed: int = 0) -> dict:
    seeds = jax.random.split(jax.random.key(seed), 16)
    tokens = bell_draw_with(seeds[0], (MB, TOKENS, D), 1.0, 6.0, ((1, 16),), (1, 2, 16, 2.0))
    lengths = jax.vmap(lambda own: uneven_parts(own, SEQS, TOK_MB, SEQ_MOST, 2))(jax.random.split(seeds[1], MB * N_DP)).reshape((MB, N_DP, SEQS)).astype(jnp.int32)
    cotangent = normal_values(seeds[2], (MB, TOKENS, D), 1.0, 6.0, ((1, 16),))
    qkv_weight = normal_values(seeds[3], (2, D, 3 * D), D ** -0.5, 0.21875, ((0, 2), (1, 16)))
    out_weight = normal_values(seeds[4], (2, D, D), (D // 16) ** -0.5, 0.875, ((0, 2), (1, 16)))
    up_weight = normal_values(seeds[5], (2, D, FF), D ** -0.5, 0.21875, ((0, 2), (1, 16)))
    down_weight = normal_values(seeds[6], (2, FF, D), FF ** -0.5, 0.109375, ((0, 2), (1, 16)))
    qkv_bias = normal_values(seeds[7], (2, 3 * D), 0.3, 1.5, ((0, 2), (1, 16)))
    out_bias = normal_values(seeds[8], (2, D), 0.3, 1.5, ((0, 2), (1, 16)))
    up_bias = normal_values(seeds[9], (2, FF), 0.3, 1.5, ((0, 2), (1, 16)))
    down_bias = normal_values(seeds[10], (2, D), 0.3, 1.5, ((0, 2), (1, 16)))
    attn_gain = jnp.clip(1.0 + 0.1 * jax.random.normal(seeds[11], (2, D), jnp.float32), 0.5, 1.5).astype(jnp.bfloat16)
    attn_shift = normal_values(seeds[12], (2, D), 0.3, 1.5, ((0, 2), (1, 16)))
    mlp_gain = jnp.clip(1.0 + 0.1 * jax.random.normal(seeds[13], (2, D), jnp.float32), 0.5, 1.5).astype(jnp.bfloat16)
    mlp_shift = normal_values(seeds[14], (2, D), 0.3, 1.5, ((0, 2), (1, 16)))
    return dict(tokens=tokens, lengths=lengths, cotangent=cotangent, qkv_weight=qkv_weight, out_weight=out_weight, up_weight=up_weight, down_weight=down_weight, qkv_bias=qkv_bias, out_bias=out_bias, up_bias=up_bias, down_bias=down_bias, attn_gain=attn_gain, attn_shift=attn_shift, mlp_gain=mlp_gain, mlp_shift=mlp_shift)


@jax.custom_vjp
def low(v):
    return lax.optimization_barrier(v.astype(jnp.bfloat16)).astype(jnp.float32)

@jax.custom_vjp
def low_back(v):
    return v

def low_keep(v):
    return (low(v), None)

def low_pass(kept, grad):
    return (grad,)

def back_keep(v):
    return (v, None)

def back_low(kept, grad):
    return (low(grad),)
low.defvjp(low_keep, low_pass)
low_back.defvjp(back_keep, back_low)
EPSILON = 1e-05
HIGHEST = lax.Precision.HIGHEST

def layer_norm(values, gain, offset):
    centre = lax.optimization_barrier(jnp.mean(values, axis=-1, keepdims=True))
    centred = values - centre
    spread = lax.optimization_barrier(jnp.mean(centred * centred, axis=-1, keepdims=True))
    return centred * lax.rsqrt(spread + EPSILON) * gain + offset

def segment_info(seq_lengths, count):
    ends = jnp.cumsum(seq_lengths).astype(jnp.int32)
    starts = (ends - seq_lengths).astype(jnp.int32)
    places = jnp.arange(count, dtype=jnp.int32)
    inside = ((places[:, None] >= starts[None, :]) & (places[:, None] < ends[None, :])).astype(jnp.int32)
    seq_ids = lax.optimization_barrier(jnp.sum(inside * jnp.arange(seq_lengths.shape[0], dtype=jnp.int32)[None, :], axis=1))
    positions = places - lax.optimization_barrier(jnp.sum(inside * starts[None, :], axis=1))
    return (seq_ids, positions)

def angle_tables(positions):
    freqs = 10000.0 ** (-jnp.arange(8, dtype=jnp.float32) / 8.0)
    angles = positions.astype(jnp.float32)[:, None] * freqs[None, :]
    return (jnp.cos(angles)[:, None, :], jnp.sin(angles)[:, None, :])

def rotate(part, cosine, sine):
    first = part[..., :8]
    second = part[..., 8:16]
    return jnp.concatenate([first * cosine - second * sine, second * cosine + first * sine, part[..., 16:]], axis=-1)

def layer_row(entry, seq_lengths, params):
    qkv_w, out_w, up_w, down_w, qkv_b, out_b, up_b, down_b, gain_a, shift_a, gain_m, shift_m = params
    count, width = entry.shape
    heads = width // 64
    seq_ids, positions = segment_info(seq_lengths, count)
    normed_a = low(layer_norm(entry, gain_a, shift_a))
    normed_m = low(layer_norm(entry, gain_m, shift_m))
    qkv = low_back(jnp.dot(normed_a, qkv_w, precision=HIGHEST) + qkv_b)
    cosine, sine = angle_tables(positions)
    queries = low(rotate(qkv[:, :width].reshape(count, heads, 64), cosine, sine))
    keys = low(rotate(qkv[:, width:2 * width].reshape(count, heads, 64), cosine, sine))
    values = low(qkv[:, 2 * width:].reshape(count, heads, 64))
    allowed = (seq_ids[:, None] == seq_ids[None, :]) & (positions[:, None] >= positions[None, :])
    scores = low_back(jnp.einsum('thd,shd->hts', queries, keys, precision=HIGHEST) * 0.125)
    scores = jnp.where(allowed[None], scores, -1e+30)
    top = lax.optimization_barrier(jnp.max(scores, axis=-1, keepdims=True))
    expo = jnp.exp(scores - top)
    weights = low(expo / lax.optimization_barrier(jnp.sum(expo, axis=-1, keepdims=True)))
    attended = jnp.einsum('hts,shd->thd', weights, values, precision=HIGHEST).reshape(count, width)
    attended = low(low_back(attended))
    hidden = low_back(jnp.dot(normed_m, up_w, precision=HIGHEST) + up_b)
    activated = low(jax.nn.gelu(hidden, approximate=False))
    branch_a = jnp.dot(attended, out_w, precision=HIGHEST) + out_b
    branch_m = jnp.dot(activated, down_w, precision=HIGHEST) + down_b
    return entry + branch_a + branch_m

def layer_all(inputs, lengths, params):
    width = inputs.shape[-1]
    rows = inputs.reshape(-1, TOK_MB, width)
    row_lengths = lengths.reshape(-1, lengths.shape[-1])
    checked = jax.checkpoint(layer_row)
    outputs = lax.map(lambda pair: checked(pair[0], pair[1], params), (rows, row_lengths))
    return outputs.reshape(inputs.shape)

def reference(tokens, lengths, cotangent, qkv_weight, out_weight, up_weight, down_weight, qkv_bias, out_bias, up_bias, down_bias, attn_gain, attn_shift, mlp_gain, mlp_shift):
    every = (qkv_weight, out_weight, up_weight, down_weight, qkv_bias, out_bias, up_bias, down_bias, attn_gain, attn_shift, mlp_gain, mlp_shift)
    first = tuple((item[0].astype(jnp.float32) for item in every))
    second = tuple((item[1].astype(jnp.float32) for item in every))

    def run_layer(inputs, params):
        return layer_all(inputs, lengths, params)
    out_first, back_first = jax.vjp(run_layer, tokens.astype(jnp.float32), first)
    entry_second = low(out_first)
    out_second, back_second = jax.vjp(run_layer, entry_second, second)
    grad_second, param_second = back_second(cotangent.astype(jnp.float32))
    grad_first, param_first = back_first(low(grad_second))
    layer_outputs = jnp.stack([entry_second, out_second]).astype(jnp.bfloat16)
    input_grads = jnp.stack([grad_first, grad_second])
    stacked = tuple((jnp.stack([left, right]) for left, right in zip(param_first, param_second)))
    return (layer_outputs, input_grads, stacked[0], stacked[1], stacked[2], stacked[3], stacked[4], stacked[5], stacked[6], stacked[7], stacked[8], stacked[9], stacked[10], stacked[11])
```

```python
import jax
import jax.numpy as jnp
from jax import lax
from jax.sharding import PartitionSpec as P

EPSILON = 1e-05
HEAD_WIDTH = 64


def layer_norm(values, gain, offset):
    centre = jnp.mean(values, axis=-1, keepdims=True)
    centred = values - centre
    spread = jnp.mean(centred * centred, axis=-1, keepdims=True)
    return centred * lax.rsqrt(spread + EPSILON) * gain + offset


def segment_info(seq_lengths, count):
    ends = jnp.cumsum(seq_lengths)
    starts = ends - seq_lengths
    places = jnp.arange(count, dtype=jnp.int32)
    inside = ((places[:, None] >= starts[None, :]) & (places[:, None] < ends[None, :])).astype(
        jnp.int32
    )
    seq_ids = jnp.sum(inside * jnp.arange(seq_lengths.shape[0], dtype=jnp.int32)[None, :], axis=1)
    positions = places - jnp.sum(inside * starts[None, :], axis=1)
    return (seq_ids, positions)


def angle_tables(positions):
    freqs = 10000.0 ** (-jnp.arange(8, dtype=jnp.float32) / 8.0)
    angles = positions.astype(jnp.float32)[:, None] * freqs[None, :]
    return (jnp.cos(angles)[:, None, :], jnp.sin(angles)[:, None, :])


def rotate(part, cosine, sine):
    first = part[..., :8]
    second = part[..., 8:16]
    return jnp.concatenate(
        [first * cosine - second * sine, second * cosine + first * sine, part[..., 16:]], axis=-1
    )


def unrotate(grad, cosine, sine):
    first = grad[..., :8]
    second = grad[..., 8:16]
    return jnp.concatenate(
        [first * cosine + second * sine, second * cosine - first * sine, grad[..., 16:]], axis=-1
    )


def layer_forward(entry, seq_lengths, gathered):
    qkv_w, out_w, up_w, down_w, qkv_b, out_b, up_b, down_b, gain_a, shift_a, gain_m, shift_m = (
        gathered
    )
    count, width = entry.shape
    heads = width // HEAD_WIDTH
    seq_ids, positions = segment_info(seq_lengths, count)
    normed_a = layer_norm(entry, gain_a.astype(jnp.float32), shift_a.astype(jnp.float32)).astype(
        jnp.bfloat16
    )
    normed_m = layer_norm(entry, gain_m.astype(jnp.float32), shift_m.astype(jnp.float32)).astype(
        jnp.bfloat16
    )
    query, key, value = (
        jnp.dot(normed_a, part, preferred_element_type=jnp.float32) + bias.astype(jnp.float32)
        for part, bias in zip(qkv_w, jnp.split(qkv_b, 3))
    )
    cosine, sine = angle_tables(positions)
    queries = rotate(query.reshape(count, heads, HEAD_WIDTH), cosine, sine).astype(
        jnp.bfloat16
    )
    keys = rotate(key.reshape(count, heads, HEAD_WIDTH), cosine, sine).astype(
        jnp.bfloat16
    )
    values = value.reshape(count, heads, HEAD_WIDTH).astype(jnp.bfloat16)
    allowed = (seq_ids[:, None] == seq_ids[None, :]) & (positions[:, None] >= positions[None, :])
    scores = jnp.einsum("thd,shd->hts", queries, keys, preferred_element_type=jnp.float32) * 0.125
    scores = jnp.where(allowed[None], scores, -1e30)
    top = jnp.max(scores, axis=-1, keepdims=True)
    expo = jnp.exp(scores - top)
    total = jnp.sum(expo, axis=-1, keepdims=True)
    log_total = top + jnp.log(total)
    weights = (expo / total).astype(jnp.bfloat16)
    attended = jnp.einsum("hts,shd->thd", weights, values, preferred_element_type=jnp.float32)
    attended = attended.reshape(count, width).astype(jnp.bfloat16)
    hidden = jnp.dot(normed_m, up_w, preferred_element_type=jnp.float32) + up_b.astype(jnp.float32)
    activated = jax.nn.gelu(hidden, approximate=False).astype(jnp.bfloat16)
    branch_a = jnp.dot(attended, out_w, preferred_element_type=jnp.float32) + out_b.astype(
        jnp.float32
    )
    branch_m = jnp.dot(activated, down_w, preferred_element_type=jnp.float32) + down_b.astype(
        jnp.float32
    )
    result = entry + branch_a + branch_m
    kept = (
        normed_a,
        normed_m,
        queries,
        keys,
        values,
        log_total,
        attended,
        hidden,
        activated,
        allowed,
        cosine,
        sine,
    )
    return (result, kept)


def layer_backward(upstream, entry, kept, gathered):
    qkv_w, out_w, up_w, down_w, qkv_b, out_b, up_b, down_b, gain_a, shift_a, gain_m, shift_m = (
        gathered
    )
    (
        normed_a,
        normed_m,
        queries,
        keys,
        values,
        log_total,
        attended,
        hidden,
        activated,
        allowed,
        cosine,
        sine,
    ) = kept
    count, width = entry.shape
    heads = width // HEAD_WIDTH
    up_low = upstream.astype(jnp.bfloat16)
    grad_down_w = jnp.einsum("tf,td->fd", activated, up_low, preferred_element_type=jnp.float32)
    grad_out_w = jnp.einsum("te,td->ed", attended, up_low, preferred_element_type=jnp.float32)
    grad_rows = jnp.sum(upstream, axis=0)
    d_activated = jnp.einsum("td,fd->tf", up_low, down_w, preferred_element_type=jnp.float32)
    _, gelu_back = jax.vjp(lambda inner: jax.nn.gelu(inner, approximate=False), hidden)
    d_hidden = gelu_back(d_activated)[0].astype(jnp.bfloat16)
    grad_up_w = jnp.einsum("td,tf->df", normed_m, d_hidden, preferred_element_type=jnp.float32)
    grad_up_b = jnp.sum(d_hidden.astype(jnp.float32), axis=0)
    d_normed_m = jnp.einsum("tf,df->td", d_hidden, up_w, preferred_element_type=jnp.float32)
    d_attended = jnp.einsum("te,de->td", up_low, out_w, preferred_element_type=jnp.float32)
    d_attended = d_attended.astype(jnp.bfloat16).reshape(count, heads, HEAD_WIDTH)
    scores = jnp.einsum("thd,shd->hts", queries, keys, preferred_element_type=jnp.float32) * 0.125
    scores = jnp.where(allowed[None], scores, -1e30)
    probs = jnp.exp(scores - log_total)
    d_probs = jnp.einsum("thd,shd->hts", d_attended, values, preferred_element_type=jnp.float32)
    d_values = jnp.einsum(
        "hts,thd->shd", probs.astype(jnp.bfloat16), d_attended, preferred_element_type=jnp.float32
    )
    d_scores = probs * (d_probs - jnp.sum(d_probs * probs, axis=-1, keepdims=True))
    d_scores = d_scores.astype(jnp.bfloat16)
    d_queries = (
        jnp.einsum("hts,shd->thd", d_scores, keys, preferred_element_type=jnp.float32) * 0.125
    )
    d_keys = (
        jnp.einsum("hts,thd->shd", d_scores, queries, preferred_element_type=jnp.float32) * 0.125
    )
    d_qkv = [
        part.reshape(count, width).astype(jnp.bfloat16)
        for part in (unrotate(d_queries, cosine, sine), unrotate(d_keys, cosine, sine), d_values)
    ]
    grad_qkv_w = [
        jnp.einsum("td,te->de", normed_a, part, preferred_element_type=jnp.float32)
        for part in d_qkv
    ]
    grad_qkv_b = jnp.concatenate([jnp.sum(part.astype(jnp.float32), axis=0) for part in d_qkv])
    d_normed_a = sum(
        jnp.einsum("te,de->td", part, weight, preferred_element_type=jnp.float32)
        for part, weight in zip(d_qkv, qkv_w)
    )
    _, norm_back_a = jax.vjp(
        layer_norm, entry, gain_a.astype(jnp.float32), shift_a.astype(jnp.float32)
    )
    d_entry_a, grad_gain_a, grad_shift_a = norm_back_a(d_normed_a)
    _, norm_back_m = jax.vjp(
        layer_norm, entry, gain_m.astype(jnp.float32), shift_m.astype(jnp.float32)
    )
    d_entry_m, grad_gain_m, grad_shift_m = norm_back_m(d_normed_m)
    d_entry = upstream + d_entry_a + d_entry_m
    grads = (
        grad_qkv_w,
        grad_out_w,
        grad_up_w,
        grad_down_w,
        grad_qkv_b,
        grad_rows,
        grad_up_b,
        grad_rows,
        grad_gain_a,
        grad_shift_a,
        grad_gain_m,
        grad_shift_m,
    )
    return (d_entry, grads)


VECTOR_ROWS = 16


def swap(value):
    return lax.ppermute(value, "section", [(0, 1), (1, 0)])


def column_blocks(shard, width):
    return jnp.concatenate(jnp.split(shard, shard.shape[1] // width, axis=1), axis=0)


def both_halves(own, core):
    other = swap(own)
    return (jnp.where(core == 0, own, other), jnp.where(core == 0, other, own))


def unpack(gathered, core, width, units):
    attn, mlp = gathered
    count = attn.shape[0]
    rows = width // count
    first, second = both_halves(attn, core)
    up, down = both_halves(mlp, core)
    square = lambda block: block.reshape(width, width)
    query, key = square(first[:, :rows]), square(first[:, rows : 2 * rows])
    value, out = square(second[:, :rows]), square(second[:, rows : 2 * rows])
    vectors = first[:, 2 * rows :].reshape(count, -1)
    small, at = [], 0
    for size in units:
        small.append(vectors[:, at : at + size * rows].reshape(size * width))
        at += size * rows
    up = up.reshape(count, -1, rows, width).transpose(0, 2, 1, 3).reshape(width, -1)
    down = down.reshape(-1, width)
    return ((query, key, value), out, up, down, *small)


def pack_vectors(vectors, count, width):
    flat = jnp.concatenate([vector.reshape(count, -1) for vector in vectors], axis=1)
    flat = jnp.pad(flat, ((0, 0), (0, VECTOR_ROWS * width - flat.shape[1])))
    return flat.reshape(count, VECTOR_ROWS, width)


def reduce_pair(low, high, core):
    arrived = swap(jnp.where(core == 0, high, low))
    own = jnp.where(core == 0, low, high)
    total = (own.astype(jnp.float32) + arrived.astype(jnp.float32)).astype(jnp.bfloat16)
    return lax.psum_scatter(total, "dp", scatter_dimension=0, tiled=False)


def reduce_mlp(grads, core, count, width):
    rows = width // count
    up = grads[2].astype(jnp.bfloat16).reshape(count, rows, -1, width)
    up = up.transpose(0, 2, 1, 3).reshape(count, -1, width)
    down = grads[3].astype(jnp.bfloat16).reshape(count, -1, width)
    return reduce_pair(up, down, core)


def reduce_attn(grads, core, count, width):
    rows = width // count
    query, key, value = (part.astype(jnp.bfloat16).reshape(count, rows, width) for part in grads[0])
    out = grads[1].astype(jnp.bfloat16).reshape(count, rows, width)
    small = pack_vectors([vector.astype(jnp.bfloat16) for vector in grads[4:]], count, width)
    low = jnp.concatenate([query, key, small], axis=1)
    high = jnp.concatenate([value, out, jnp.zeros_like(small)], axis=1)
    return reduce_pair(low, high, core)


def on_device(
    tokens,
    lengths,
    cotangent,
    qkv_weight,
    out_weight,
    up_weight,
    down_weight,
    qkv_bias,
    out_bias,
    up_bias,
    down_bias,
    attn_gain,
    attn_shift,
    mlp_gain,
    mlp_shift,
):
    core = lax.axis_index("section")
    count = lax.axis_size("dp")
    width = tokens.shape[2]
    rows = width // count
    vectors = (
        qkv_bias[0],
        out_bias[0],
        up_bias[0],
        down_bias[0],
        attn_gain[0],
        attn_shift[0],
        mlp_gain[0],
        mlp_shift[0],
    )
    units = [vector.shape[0] // rows for vector in vectors]
    qkv_blocks = column_blocks(qkv_weight[0], width)
    small = pack_vectors([vector[None] for vector in vectors], 1, width)[0]
    attn_low = jnp.concatenate([qkv_blocks[: 2 * rows], small], axis=0)
    attn_high = jnp.concatenate(
        [qkv_blocks[2 * rows :], out_weight[0], jnp.zeros_like(small)], axis=0
    )
    mlp_low = column_blocks(up_weight[0], width)
    mlp_high = down_weight[0]
    pieces = []
    for low, high in ((attn_low, attn_high), (mlp_low, mlp_high)):
        arrived = swap(jnp.where(core == 0, high, low))
        own = jnp.where(core == 0, low, high)
        pieces.append((jnp.where(core == 0, own, arrived), jnp.where(core == 0, arrived, own)))
    gathered = [
        tuple(lax.all_gather(piece[layer], "dp", axis=0, tiled=False) for piece in pieces)
        for layer in range(2)
    ]
    parameters = [unpack(gathered[layer], core, width, units) for layer in range(2)]

    seq_lengths = lax.dynamic_index_in_dim(lengths, core, 0, keepdims=False)[0]
    entry = lax.dynamic_index_in_dim(tokens, core, 0, keepdims=False).astype(jnp.float32)
    entries, keeps, results = ([], [], [])
    for layer in range(2):
        result, kept = layer_forward(entry, seq_lengths, parameters[layer])
        rounded = result.astype(jnp.bfloat16)
        entries.append(entry)
        keeps.append(kept)
        results.append(rounded)
        entry = rounded.astype(jnp.float32)

    def by_layer(first, second):
        own = jnp.where(core == 0, first, second)
        arrived = swap(jnp.where(core == 0, second, first))
        return jnp.stack(
            [jnp.where(core == 0, own, arrived), jnp.where(core == 0, arrived, own)]
        )

    layer_outputs = by_layer(*results)
    upstream = lax.dynamic_index_in_dim(cotangent, core, 0, keepdims=False).astype(jnp.float32)
    backs, mlps, attns = ([None, None], [None, None], [None, None])
    for layer in (1, 0):
        d_entry, grads = layer_backward(upstream, entries[layer], keeps[layer], parameters[layer])
        backs[layer] = d_entry
        mlps[layer] = reduce_mlp(grads, core, count, width)
        attns[layer] = reduce_attn(grads, core, count, width)
        upstream = d_entry.astype(jnp.bfloat16).astype(jnp.float32)
    input_grads = by_layer(*backs)
    mlp_low, mlp_high = by_layer(*mlps).astype(jnp.float32)
    attn_low, attn_high = by_layer(*attns).astype(jnp.float32)
    grad_qkv = jnp.concatenate(
        [attn_low[:rows], attn_low[rows : 2 * rows], attn_high[:rows]], axis=1
    )
    grad_out = attn_high[rows : 2 * rows]
    grad_up = jnp.concatenate(jnp.split(mlp_low, mlp_low.shape[0] // rows, axis=0), axis=1)
    flat = attn_low[2 * rows :].reshape(-1)
    reduced, at = [grad_qkv, grad_out, grad_up, mlp_high], 0
    for size in units:
        reduced.append(flat[at : at + size * rows])
        at += size * rows
    return (layer_outputs[None], input_grads[None]) + tuple((piece[None] for piece in reduced))


def solution(mesh):
    placed = (
        P(None, "dp", None),
        P(None, "dp", None),
        P(None, "dp", None),
        P("section", "dp", None),
        P("section", "dp", None),
        P("section", "dp", None),
        P("section", "dp", None),
        P("section", "dp"),
        P("section", "dp"),
        P("section", "dp"),
        P("section", "dp"),
        P("section", "dp"),
        P("section", "dp"),
        P("section", "dp"),
        P("section", "dp"),
    )
    return jax.shard_map(
        on_device,
        mesh=mesh,
        in_specs=placed,
        out_specs=(
            P("section", None, "dp", None),
            P("section", None, "dp", None),
            P("section", "dp", None),
            P("section", "dp", None),
            P("section", "dp", None),
            P("section", "dp", None),
            P("section", "dp"),
            P("section", "dp"),
            P("section", "dp"),
            P("section", "dp"),
            P("section", "dp"),
            P("section", "dp"),
            P("section", "dp"),
            P("section", "dp"),
        ),
        check_vma=False,
    )
```

```python
import jax
import jax.numpy as jnp
from jax import lax
from jax.sharding import PartitionSpec as P

EPSILON = 1e-05
HEAD_WIDTH = 64


def layer_norm(values, gain, offset):
    centre = jnp.mean(values, axis=-1, keepdims=True)
    centred = values - centre
    spread = jnp.mean(centred * centred, axis=-1, keepdims=True)
    return centred * lax.rsqrt(spread + EPSILON) * gain + offset


def segment_info(seq_lengths, count):
    ends = jnp.cumsum(seq_lengths)
    starts = ends - seq_lengths
    places = jnp.arange(count, dtype=jnp.int32)
    inside = ((places[:, None] >= starts[None, :]) & (places[:, None] < ends[None, :])).astype(
        jnp.int32
    )
    seq_ids = jnp.sum(inside * jnp.arange(seq_lengths.shape[0], dtype=jnp.int32)[None, :], axis=1)
    positions = places - jnp.sum(inside * starts[None, :], axis=1)
    return (seq_ids, positions)


def angle_tables(positions):
    freqs = 10000.0 ** (-jnp.arange(8, dtype=jnp.float32) / 8.0)
    angles = positions.astype(jnp.float32)[:, None] * freqs[None, :]
    return (jnp.cos(angles)[:, None, :], jnp.sin(angles)[:, None, :])


def rotate(part, cosine, sine):
    first = part[..., :8]
    second = part[..., 8:16]
    return jnp.concatenate(
        [first * cosine - second * sine, second * cosine + first * sine, part[..., 16:]], axis=-1
    )


def unrotate(grad, cosine, sine):
    first = grad[..., :8]
    second = grad[..., 8:16]
    return jnp.concatenate(
        [first * cosine + second * sine, second * cosine - first * sine, grad[..., 16:]], axis=-1
    )


def layer_forward(entry, seq_lengths, gathered):
    qkv_w, out_w, up_w, down_w, qkv_b, out_b, up_b, down_b, gain_a, shift_a, gain_m, shift_m = (
        gathered
    )
    count, width = entry.shape
    heads = width // HEAD_WIDTH
    seq_ids, positions = segment_info(seq_lengths, count)
    normed_a = layer_norm(entry, gain_a.astype(jnp.float32), shift_a.astype(jnp.float32)).astype(
        jnp.bfloat16
    )
    normed_m = layer_norm(entry, gain_m.astype(jnp.float32), shift_m.astype(jnp.float32)).astype(
        jnp.bfloat16
    )
    query, key, value = (
        jnp.dot(normed_a, part, preferred_element_type=jnp.float32) + bias.astype(jnp.float32)
        for part, bias in zip(qkv_w, jnp.split(qkv_b, 3))
    )
    cosine, sine = angle_tables(positions)
    queries = rotate(query.reshape(count, heads, HEAD_WIDTH), cosine, sine).astype(
        jnp.bfloat16
    )
    keys = rotate(key.reshape(count, heads, HEAD_WIDTH), cosine, sine).astype(
        jnp.bfloat16
    )
    values = value.reshape(count, heads, HEAD_WIDTH).astype(jnp.bfloat16)
    allowed = (seq_ids[:, None] == seq_ids[None, :]) & (positions[:, None] >= positions[None, :])
    scores = jnp.einsum("thd,shd->hts", queries, keys, preferred_element_type=jnp.float32) * 0.125
    scores = jnp.where(allowed[None], scores, -1e30)
    top = jnp.max(scores, axis=-1, keepdims=True)
    expo = jnp.exp(scores - top)
    total = jnp.sum(expo, axis=-1, keepdims=True)
    log_total = top + jnp.log(total)
    weights = (expo / total).astype(jnp.bfloat16)
    attended = jnp.einsum("hts,shd->thd", weights, values, preferred_element_type=jnp.float32)
    attended = attended.reshape(count, width).astype(jnp.bfloat16)
    hidden = jnp.dot(normed_m, up_w, preferred_element_type=jnp.float32) + up_b.astype(jnp.float32)
    activated = jax.nn.gelu(hidden, approximate=False).astype(jnp.bfloat16)
    branch_a = jnp.dot(attended, out_w, preferred_element_type=jnp.float32) + out_b.astype(
        jnp.float32
    )
    branch_m = jnp.dot(activated, down_w, preferred_element_type=jnp.float32) + down_b.astype(
        jnp.float32
    )
    result = entry + branch_a + branch_m
    kept = (
        normed_a,
        normed_m,
        queries,
        keys,
        values,
        log_total,
        attended,
        hidden,
        activated,
        allowed,
        cosine,
        sine,
    )
    return (result, kept)


def layer_backward(upstream, entry, kept, gathered):
    qkv_w, out_w, up_w, down_w, qkv_b, out_b, up_b, down_b, gain_a, shift_a, gain_m, shift_m = (
        gathered
    )
    (
        normed_a,
        normed_m,
        queries,
        keys,
        values,
        log_total,
        attended,
        hidden,
        activated,
        allowed,
        cosine,
        sine,
    ) = kept
    count, width = entry.shape
    heads = width // HEAD_WIDTH
    up_low = upstream.astype(jnp.bfloat16)
    grad_down_w = jnp.einsum("tf,td->fd", activated, up_low, preferred_element_type=jnp.float32)
    grad_out_w = jnp.einsum("te,td->ed", attended, up_low, preferred_element_type=jnp.float32)
    grad_rows = jnp.sum(upstream, axis=0)
    d_activated = jnp.einsum("td,fd->tf", up_low, down_w, preferred_element_type=jnp.float32)
    _, gelu_back = jax.vjp(lambda inner: jax.nn.gelu(inner, approximate=False), hidden)
    d_hidden = gelu_back(d_activated)[0].astype(jnp.bfloat16)
    grad_up_w = jnp.einsum("td,tf->df", normed_m, d_hidden, preferred_element_type=jnp.float32)
    grad_up_b = jnp.sum(d_hidden.astype(jnp.float32), axis=0)
    d_normed_m = jnp.einsum("tf,df->td", d_hidden, up_w, preferred_element_type=jnp.float32)
    d_attended = jnp.einsum("te,de->td", up_low, out_w, preferred_element_type=jnp.float32)
    d_attended = d_attended.astype(jnp.bfloat16).reshape(count, heads, HEAD_WIDTH)
    scores = jnp.einsum("thd,shd->hts", queries, keys, preferred_element_type=jnp.float32) * 0.125
    scores = jnp.where(allowed[None], scores, -1e30)
    probs = jnp.exp(scores - log_total)
    d_probs = jnp.einsum("thd,shd->hts", d_attended, values, preferred_element_type=jnp.float32)
    d_values = jnp.einsum(
        "hts,thd->shd", probs.astype(jnp.bfloat16), d_attended, preferred_element_type=jnp.float32
    )
    d_scores = probs * (d_probs - jnp.sum(d_probs * probs, axis=-1, keepdims=True))
    d_scores = d_scores.astype(jnp.bfloat16)
    d_queries = (
        jnp.einsum("hts,shd->thd", d_scores, keys, preferred_element_type=jnp.float32) * 0.125
    )
    d_keys = (
        jnp.einsum("hts,thd->shd", d_scores, queries, preferred_element_type=jnp.float32) * 0.125
    )
    d_qkv = [
        part.reshape(count, width).astype(jnp.bfloat16)
        for part in (unrotate(d_queries, cosine, sine), unrotate(d_keys, cosine, sine), d_values)
    ]
    grad_qkv_w = [
        jnp.einsum("td,te->de", normed_a, part, preferred_element_type=jnp.float32)
        for part in d_qkv
    ]
    grad_qkv_b = jnp.concatenate([jnp.sum(part.astype(jnp.float32), axis=0) for part in d_qkv])
    d_normed_a = sum(
        jnp.einsum("te,de->td", part, weight, preferred_element_type=jnp.float32)
        for part, weight in zip(d_qkv, qkv_w)
    )
    _, norm_back_a = jax.vjp(
        layer_norm, entry, gain_a.astype(jnp.float32), shift_a.astype(jnp.float32)
    )
    d_entry_a, grad_gain_a, grad_shift_a = norm_back_a(d_normed_a)
    _, norm_back_m = jax.vjp(
        layer_norm, entry, gain_m.astype(jnp.float32), shift_m.astype(jnp.float32)
    )
    d_entry_m, grad_gain_m, grad_shift_m = norm_back_m(d_normed_m)
    d_entry = upstream + d_entry_a + d_entry_m
    grads = (
        grad_qkv_w,
        grad_out_w,
        grad_up_w,
        grad_down_w,
        grad_qkv_b,
        grad_rows,
        grad_up_b,
        grad_rows,
        grad_gain_a,
        grad_shift_a,
        grad_gain_m,
        grad_shift_m,
    )
    return (d_entry, grads)


VECTOR_ROWS = 16


def swap(value):
    return lax.ppermute(value, "section", [(0, 1), (1, 0)])


def link_orders(count):
    bits = list(range(count.bit_length() - 1))
    near, far = bits[:3], bits[3:]
    return [near[turn:] + near[:turn] + far for turn in range(max(1, len(near)))]


def row_parts(height, parts):
    step = 8 * -(-height // (8 * parts))
    edges = [min(height, step * part) for part in range(parts + 1)]
    return [(low, high) for low, high in zip(edges, edges[1:]) if high > low]


def exchange(value, bit, count):
    return lax.ppermute(value, "dp", [(source, source ^ (1 << bit)) for source in range(count)])


def gather_dp(piece, count):
    orders = link_orders(count)
    places = count.bit_length() - 1
    me = lax.axis_index("dp")
    done = []
    for (low, high), order in zip(row_parts(piece.shape[0], len(orders)), orders):
        held = piece[low:high].reshape((1,) * places + (high - low, piece.shape[1]))
        for bit in reversed(order):
            other = exchange(held, bit, count)
            axis = places - 1 - bit
            mine = (me >> bit) & 1
            held = jnp.where(
                mine == 0,
                jnp.concatenate([held, other], axis=axis),
                jnp.concatenate([other, held], axis=axis),
            )
        done.append(held.reshape(count, high - low, piece.shape[1]))
    return jnp.concatenate(done, axis=1)


def scatter_sum_dp(whole, count):
    orders = link_orders(count)
    places = count.bit_length() - 1
    me = lax.axis_index("dp")
    done = []
    for (low, high), order in zip(row_parts(whole.shape[1], len(orders)), orders):
        held = whole[:, low:high].reshape((2,) * places + (high - low, whole.shape[2]))
        for bit in order:
            axis = places - 1 - bit
            mine = (me >> bit) & 1
            sent = lax.dynamic_index_in_dim(held, 1 - mine, axis, keepdims=True)
            kept = lax.dynamic_index_in_dim(held, mine, axis, keepdims=True)
            arrived = exchange(sent, bit, count)
            held = (kept.astype(jnp.float32) + arrived.astype(jnp.float32)).astype(jnp.bfloat16)
        done.append(held.reshape(high - low, whole.shape[2]))
    return jnp.concatenate(done, axis=0)


def column_blocks(shard, width):
    return jnp.concatenate(jnp.split(shard, shard.shape[1] // width, axis=1), axis=0)


def both_halves(own, core):
    other = swap(own)
    return (jnp.where(core == 0, own, other), jnp.where(core == 0, other, own))


def unpack(gathered, core, width, units):
    attn, mlp = gathered
    count = attn.shape[0]
    rows = width // count
    first, second = both_halves(attn, core)
    up, down = both_halves(mlp, core)
    square = lambda block: block.reshape(width, width)
    query, key = square(first[:, :rows]), square(first[:, rows : 2 * rows])
    value, out = square(second[:, :rows]), square(second[:, rows : 2 * rows])
    vectors = first[:, 2 * rows :].reshape(count, -1)
    small, at = [], 0
    for size in units:
        small.append(vectors[:, at : at + size * rows].reshape(size * width))
        at += size * rows
    up = up.reshape(count, -1, rows, width).transpose(0, 2, 1, 3).reshape(width, -1)
    down = down.reshape(-1, width)
    return ((query, key, value), out, up, down, *small)


def pack_vectors(vectors, count, width):
    flat = jnp.concatenate([vector.reshape(count, -1) for vector in vectors], axis=1)
    flat = jnp.pad(flat, ((0, 0), (0, VECTOR_ROWS * width - flat.shape[1])))
    return flat.reshape(count, VECTOR_ROWS, width)


def reduce_pair(low, high, core):
    arrived = swap(jnp.where(core == 0, high, low))
    own = jnp.where(core == 0, low, high)
    total = (own.astype(jnp.float32) + arrived.astype(jnp.float32)).astype(jnp.bfloat16)
    return scatter_sum_dp(total, total.shape[0])


def reduce_mlp(grads, core, count, width):
    rows = width // count
    up = grads[2].astype(jnp.bfloat16).reshape(count, rows, -1, width)
    up = up.transpose(0, 2, 1, 3).reshape(count, -1, width)
    down = grads[3].astype(jnp.bfloat16).reshape(count, -1, width)
    return reduce_pair(up, down, core)


def reduce_attn(grads, core, count, width):
    rows = width // count
    query, key, value = (part.astype(jnp.bfloat16).reshape(count, rows, width) for part in grads[0])
    out = grads[1].astype(jnp.bfloat16).reshape(count, rows, width)
    small = pack_vectors([vector.astype(jnp.bfloat16) for vector in grads[4:]], count, width)
    low = jnp.concatenate([query, key, small], axis=1)
    high = jnp.concatenate([value, out, jnp.zeros_like(small)], axis=1)
    return reduce_pair(low, high, core)


def on_device(
    tokens,
    lengths,
    cotangent,
    qkv_weight,
    out_weight,
    up_weight,
    down_weight,
    qkv_bias,
    out_bias,
    up_bias,
    down_bias,
    attn_gain,
    attn_shift,
    mlp_gain,
    mlp_shift,
):
    core = lax.axis_index("section")
    count = lax.axis_size("dp")
    width = tokens.shape[2]
    rows = width // count
    vectors = (
        qkv_bias[0],
        out_bias[0],
        up_bias[0],
        down_bias[0],
        attn_gain[0],
        attn_shift[0],
        mlp_gain[0],
        mlp_shift[0],
    )
    units = [vector.shape[0] // rows for vector in vectors]
    qkv_blocks = column_blocks(qkv_weight[0], width)
    small = pack_vectors([vector[None] for vector in vectors], 1, width)[0]
    attn_low = jnp.concatenate([qkv_blocks[: 2 * rows], small], axis=0)
    attn_high = jnp.concatenate(
        [qkv_blocks[2 * rows :], out_weight[0], jnp.zeros_like(small)], axis=0
    )
    mlp_low = column_blocks(up_weight[0], width)
    mlp_high = down_weight[0]
    pieces = []
    for low, high in ((attn_low, attn_high), (mlp_low, mlp_high)):
        arrived = swap(jnp.where(core == 0, high, low))
        own = jnp.where(core == 0, low, high)
        pieces.append((jnp.where(core == 0, own, arrived), jnp.where(core == 0, arrived, own)))
    gathered = [
        tuple(gather_dp(piece[layer], count) for piece in pieces)
        for layer in range(2)
    ]
    parameters = [unpack(gathered[layer], core, width, units) for layer in range(2)]

    seq_lengths = lax.dynamic_index_in_dim(lengths, core, 0, keepdims=False)[0]
    entry = lax.dynamic_index_in_dim(tokens, core, 0, keepdims=False).astype(jnp.float32)
    entries, keeps, results = ([], [], [])
    for layer in range(2):
        result, kept = layer_forward(entry, seq_lengths, parameters[layer])
        rounded = result.astype(jnp.bfloat16)
        entries.append(entry)
        keeps.append(kept)
        results.append(rounded)
        entry = rounded.astype(jnp.float32)

    def by_layer(first, second):
        own = jnp.where(core == 0, first, second)
        arrived = swap(jnp.where(core == 0, second, first))
        return jnp.stack(
            [jnp.where(core == 0, own, arrived), jnp.where(core == 0, arrived, own)]
        )

    layer_outputs = by_layer(*results)
    upstream = lax.dynamic_index_in_dim(cotangent, core, 0, keepdims=False).astype(jnp.float32)
    backs, mlps, attns = ([None, None], [None, None], [None, None])
    for layer in (1, 0):
        d_entry, grads = layer_backward(upstream, entries[layer], keeps[layer], parameters[layer])
        backs[layer] = d_entry
        mlps[layer] = reduce_mlp(grads, core, count, width)
        attns[layer] = reduce_attn(grads, core, count, width)
        upstream = d_entry.astype(jnp.bfloat16).astype(jnp.float32)
    input_grads = by_layer(*backs)
    mlp_low, mlp_high = by_layer(*mlps).astype(jnp.float32)
    attn_low, attn_high = by_layer(*attns).astype(jnp.float32)
    grad_qkv = jnp.concatenate(
        [attn_low[:rows], attn_low[rows : 2 * rows], attn_high[:rows]], axis=1
    )
    grad_out = attn_high[rows : 2 * rows]
    grad_up = jnp.concatenate(jnp.split(mlp_low, mlp_low.shape[0] // rows, axis=0), axis=1)
    flat = attn_low[2 * rows :].reshape(-1)
    reduced, at = [grad_qkv, grad_out, grad_up, mlp_high], 0
    for size in units:
        reduced.append(flat[at : at + size * rows])
        at += size * rows
    return (layer_outputs[None], input_grads[None]) + tuple((piece[None] for piece in reduced))


def solution(mesh):
    placed = (
        P(None, "dp", None),
        P(None, "dp", None),
        P(None, "dp", None),
        P("section", "dp", None),
        P("section", "dp", None),
        P("section", "dp", None),
        P("section", "dp", None),
        P("section", "dp"),
        P("section", "dp"),
        P("section", "dp"),
        P("section", "dp"),
        P("section", "dp"),
        P("section", "dp"),
        P("section", "dp"),
        P("section", "dp"),
    )
    return jax.shard_map(
        on_device,
        mesh=mesh,
        in_specs=placed,
        out_specs=(
            P("section", None, "dp", None),
            P("section", None, "dp", None),
            P("section", "dp", None),
            P("section", "dp", None),
            P("section", "dp", None),
            P("section", "dp", None),
            P("section", "dp"),
            P("section", "dp"),
            P("section", "dp"),
            P("section", "dp"),
            P("section", "dp"),
            P("section", "dp"),
            P("section", "dp"),
            P("section", "dp"),
        ),
        check_vma=False,
    )
```

```python
import jax
import jax.numpy as jnp
from jax import lax
from jax.sharding import PartitionSpec as P

EPSILON = 1e-05
HEAD_WIDTH = 64


def layer_norm(values, gain, offset):
    centre = jnp.mean(values, axis=-1, keepdims=True)
    centred = values - centre
    spread = jnp.mean(centred * centred, axis=-1, keepdims=True)
    return centred * lax.rsqrt(spread + EPSILON) * gain + offset


def segment_info(seq_lengths, count):
    ends = jnp.cumsum(seq_lengths)
    starts = ends - seq_lengths
    places = jnp.arange(count, dtype=jnp.int32)
    inside = ((places[:, None] >= starts[None, :]) & (places[:, None] < ends[None, :])).astype(
        jnp.int32
    )
    seq_ids = jnp.sum(inside * jnp.arange(seq_lengths.shape[0], dtype=jnp.int32)[None, :], axis=1)
    positions = places - jnp.sum(inside * starts[None, :], axis=1)
    return (seq_ids, positions)


def angle_tables(positions):
    freqs = 10000.0 ** (-jnp.arange(8, dtype=jnp.float32) / 8.0)
    angles = positions.astype(jnp.float32)[:, None] * freqs[None, :]
    return (jnp.cos(angles)[:, None, :], jnp.sin(angles)[:, None, :])


def rotate(part, cosine, sine):
    first = part[..., :8]
    second = part[..., 8:16]
    return jnp.concatenate(
        [first * cosine - second * sine, second * cosine + first * sine, part[..., 16:]], axis=-1
    )


def unrotate(grad, cosine, sine):
    first = grad[..., :8]
    second = grad[..., 8:16]
    return jnp.concatenate(
        [first * cosine + second * sine, second * cosine - first * sine, grad[..., 16:]], axis=-1
    )


def layer_forward(entry, seq_lengths, gathered):
    qkv_w, out_w, up_w, down_w, qkv_b, out_b, up_b, down_b, gain_a, shift_a, gain_m, shift_m = (
        gathered
    )
    count, width = entry.shape
    heads = width // HEAD_WIDTH
    seq_ids, positions = segment_info(seq_lengths, count)
    normed_a = layer_norm(entry, gain_a.astype(jnp.float32), shift_a.astype(jnp.float32)).astype(
        jnp.bfloat16
    )
    normed_m = layer_norm(entry, gain_m.astype(jnp.float32), shift_m.astype(jnp.float32)).astype(
        jnp.bfloat16
    )
    query, key, value = (
        jnp.dot(normed_a, part, preferred_element_type=jnp.float32) + bias.astype(jnp.float32)
        for part, bias in zip(qkv_w, jnp.split(qkv_b, 3))
    )
    cosine, sine = angle_tables(positions)
    queries = rotate(query.reshape(count, heads, HEAD_WIDTH), cosine, sine).astype(
        jnp.bfloat16
    )
    keys = rotate(key.reshape(count, heads, HEAD_WIDTH), cosine, sine).astype(
        jnp.bfloat16
    )
    values = value.reshape(count, heads, HEAD_WIDTH).astype(jnp.bfloat16)
    allowed = (seq_ids[:, None] == seq_ids[None, :]) & (positions[:, None] >= positions[None, :])
    scores = jnp.einsum("thd,shd->hts", queries, keys, preferred_element_type=jnp.float32) * 0.125
    scores = jnp.where(allowed[None], scores, -1e30)
    top = jnp.max(scores, axis=-1, keepdims=True)
    expo = jnp.exp(scores - top)
    total = jnp.sum(expo, axis=-1, keepdims=True)
    log_total = top + jnp.log(total)
    weights = (expo / total).astype(jnp.bfloat16)
    attended = jnp.einsum("hts,shd->thd", weights, values, preferred_element_type=jnp.float32)
    attended = attended.reshape(count, width).astype(jnp.bfloat16)
    hidden = jnp.dot(normed_m, up_w, preferred_element_type=jnp.float32) + up_b.astype(jnp.float32)
    activated = jax.nn.gelu(hidden, approximate=False).astype(jnp.bfloat16)
    branch_a = jnp.dot(attended, out_w, preferred_element_type=jnp.float32) + out_b.astype(
        jnp.float32
    )
    branch_m = jnp.dot(activated, down_w, preferred_element_type=jnp.float32) + down_b.astype(
        jnp.float32
    )
    result = entry + branch_a + branch_m
    kept = (
        normed_a,
        normed_m,
        queries,
        keys,
        values,
        log_total,
        attended,
        hidden,
        activated,
        allowed,
        cosine,
        sine,
    )
    return (result, kept)


def layer_backward(upstream, entry, kept, gathered):
    qkv_w, out_w, up_w, down_w, qkv_b, out_b, up_b, down_b, gain_a, shift_a, gain_m, shift_m = (
        gathered
    )
    (
        normed_a,
        normed_m,
        queries,
        keys,
        values,
        log_total,
        attended,
        hidden,
        activated,
        allowed,
        cosine,
        sine,
    ) = kept
    count, width = entry.shape
    heads = width // HEAD_WIDTH
    up_low = upstream.astype(jnp.bfloat16)
    grad_down_w = jnp.einsum("tf,td->fd", activated, up_low, preferred_element_type=jnp.float32)
    grad_out_w = jnp.einsum("te,td->ed", attended, up_low, preferred_element_type=jnp.float32)
    grad_rows = jnp.sum(upstream, axis=0)
    d_activated = jnp.einsum("td,fd->tf", up_low, down_w, preferred_element_type=jnp.float32)
    _, gelu_back = jax.vjp(lambda inner: jax.nn.gelu(inner, approximate=False), hidden)
    d_hidden = gelu_back(d_activated)[0].astype(jnp.bfloat16)
    grad_up_w = jnp.einsum("td,tf->df", normed_m, d_hidden, preferred_element_type=jnp.float32)
    grad_up_b = jnp.sum(d_hidden.astype(jnp.float32), axis=0)
    d_normed_m = jnp.einsum("tf,df->td", d_hidden, up_w, preferred_element_type=jnp.float32)
    d_attended = jnp.einsum("te,de->td", up_low, out_w, preferred_element_type=jnp.float32)
    d_attended = d_attended.astype(jnp.bfloat16).reshape(count, heads, HEAD_WIDTH)
    scores = jnp.einsum("thd,shd->hts", queries, keys, preferred_element_type=jnp.float32) * 0.125
    scores = jnp.where(allowed[None], scores, -1e30)
    probs = jnp.exp(scores - log_total)
    d_probs = jnp.einsum("thd,shd->hts", d_attended, values, preferred_element_type=jnp.float32)
    d_values = jnp.einsum(
        "hts,thd->shd", probs.astype(jnp.bfloat16), d_attended, preferred_element_type=jnp.float32
    )
    d_scores = probs * (d_probs - jnp.sum(d_probs * probs, axis=-1, keepdims=True))
    d_scores = d_scores.astype(jnp.bfloat16)
    d_queries = (
        jnp.einsum("hts,shd->thd", d_scores, keys, preferred_element_type=jnp.float32) * 0.125
    )
    d_keys = (
        jnp.einsum("hts,thd->shd", d_scores, queries, preferred_element_type=jnp.float32) * 0.125
    )
    d_qkv = [
        part.reshape(count, width).astype(jnp.bfloat16)
        for part in (unrotate(d_queries, cosine, sine), unrotate(d_keys, cosine, sine), d_values)
    ]
    grad_qkv_w = [
        jnp.einsum("td,te->de", normed_a, part, preferred_element_type=jnp.float32)
        for part in d_qkv
    ]
    grad_qkv_b = jnp.concatenate([jnp.sum(part.astype(jnp.float32), axis=0) for part in d_qkv])
    d_normed_a = sum(
        jnp.einsum("te,de->td", part, weight, preferred_element_type=jnp.float32)
        for part, weight in zip(d_qkv, qkv_w)
    )
    _, norm_back_a = jax.vjp(
        layer_norm, entry, gain_a.astype(jnp.float32), shift_a.astype(jnp.float32)
    )
    d_entry_a, grad_gain_a, grad_shift_a = norm_back_a(d_normed_a)
    _, norm_back_m = jax.vjp(
        layer_norm, entry, gain_m.astype(jnp.float32), shift_m.astype(jnp.float32)
    )
    d_entry_m, grad_gain_m, grad_shift_m = norm_back_m(d_normed_m)
    d_entry = upstream + d_entry_a + d_entry_m
    grads = (
        grad_qkv_w,
        grad_out_w,
        grad_up_w,
        grad_down_w,
        grad_qkv_b,
        grad_rows,
        grad_up_b,
        grad_rows,
        grad_gain_a,
        grad_shift_a,
        grad_gain_m,
        grad_shift_m,
    )
    return (d_entry, grads)


VECTOR_ROWS = 16


def swap(value):
    return lax.ppermute(value, "section", [(0, 1), (1, 0)])


def link_orders(count):
    bits = list(range(count.bit_length() - 1))
    near, far = bits[:3], bits[3:]
    return [near[turn:] + near[:turn] + far for turn in range(max(1, len(near)))]


def row_parts(height, parts):
    step = 8 * -(-height // (8 * parts))
    edges = [min(height, step * part) for part in range(parts + 1)]
    return [(low, high) for low, high in zip(edges, edges[1:]) if high > low]


def exchange(value, bit, count):
    return lax.ppermute(value, "dp", [(source, source ^ (1 << bit)) for source in range(count)])


def gather_dp(piece, count):
    orders = link_orders(count)
    places = count.bit_length() - 1
    me = lax.axis_index("dp")
    done = []
    for (low, high), order in zip(row_parts(piece.shape[0], len(orders)), orders):
        held = piece[low:high].reshape((1,) * places + (high - low, piece.shape[1]))
        for bit in reversed(order):
            other = exchange(held, bit, count)
            axis = places - 1 - bit
            mine = (me >> bit) & 1
            held = jnp.where(
                mine == 0,
                jnp.concatenate([held, other], axis=axis),
                jnp.concatenate([other, held], axis=axis),
            )
        done.append(held.reshape(count, high - low, piece.shape[1]))
    return jnp.concatenate(done, axis=1)


def scatter_sum_dp(whole, count):
    orders = link_orders(count)
    places = count.bit_length() - 1
    me = lax.axis_index("dp")
    done = []
    for (low, high), order in zip(row_parts(whole.shape[1], len(orders)), orders):
        held = whole[:, low:high].reshape((2,) * places + (high - low, whole.shape[2]))
        for bit in order:
            axis = places - 1 - bit
            mine = (me >> bit) & 1
            sent = lax.dynamic_index_in_dim(held, 1 - mine, axis, keepdims=True)
            kept = lax.dynamic_index_in_dim(held, mine, axis, keepdims=True)
            arrived = exchange(sent, bit, count)
            held = (kept.astype(jnp.float32) + arrived.astype(jnp.float32)).astype(jnp.bfloat16)
        done.append(held.reshape(high - low, whole.shape[2]))
    return jnp.concatenate(done, axis=0)


def column_blocks(shard, width):
    return jnp.concatenate(jnp.split(shard, shard.shape[1] // width, axis=1), axis=0)


def both_halves(own, core):
    other = swap(own)
    return (jnp.where(core == 0, own, other), jnp.where(core == 0, other, own))


def unpack(gathered, core, width, units):
    attn, mlp = gathered
    count = attn.shape[0]
    rows = width // count
    first, second = both_halves(attn, core)
    up, down = both_halves(mlp, core)
    square = lambda block: block.reshape(width, width)
    query, key = square(first[:, :rows]), square(first[:, rows : 2 * rows])
    value, out = square(second[:, :rows]), square(second[:, rows : 2 * rows])
    vectors = first[:, 2 * rows :].reshape(count, -1)
    small, at = [], 0
    for size in units:
        small.append(vectors[:, at : at + size * rows].reshape(size * width))
        at += size * rows
    up = jnp.concatenate(
        [square(up[:, at : at + rows]) for at in range(0, up.shape[1], rows)], axis=1
    )
    down = down.reshape(-1, width)
    return ((query, key, value), out, up, down, *small)


def pack_vectors(vectors, count, width):
    flat = jnp.concatenate([vector.reshape(count, -1) for vector in vectors], axis=1)
    flat = jnp.pad(flat, ((0, 0), (0, VECTOR_ROWS * width - flat.shape[1])))
    return flat.reshape(count, VECTOR_ROWS, width)


def pair_total(low, high, core):
    arrived = swap(jnp.where(core == 0, high, low))
    own = jnp.where(core == 0, low, high)
    return (own.astype(jnp.float32) + arrived.astype(jnp.float32)).astype(jnp.bfloat16)


def mlp_pair(grads, count, width):
    rows = width // count
    up = jnp.concatenate(
        [
            block.reshape(count, rows, width)
            for block in jnp.split(grads[2].astype(jnp.bfloat16), grads[2].shape[1] // width, axis=1)
        ],
        axis=1,
    )
    down = grads[3].astype(jnp.bfloat16).reshape(count, -1, width)
    return up, down


def attn_pair(grads, count, width):
    rows = width // count
    query, key, value = (part.astype(jnp.bfloat16).reshape(count, rows, width) for part in grads[0])
    out = grads[1].astype(jnp.bfloat16).reshape(count, rows, width)
    small = pack_vectors([vector.astype(jnp.bfloat16) for vector in grads[4:]], count, width)
    low = jnp.concatenate([query, key, small], axis=1)
    high = jnp.concatenate([value, out, jnp.zeros_like(small)], axis=1)
    return low, high


def on_device(
    tokens,
    lengths,
    cotangent,
    qkv_weight,
    out_weight,
    up_weight,
    down_weight,
    qkv_bias,
    out_bias,
    up_bias,
    down_bias,
    attn_gain,
    attn_shift,
    mlp_gain,
    mlp_shift,
):
    core = lax.axis_index("section")
    count = lax.axis_size("dp")
    width = tokens.shape[2]
    rows = width // count
    vectors = (
        qkv_bias[0],
        out_bias[0],
        up_bias[0],
        down_bias[0],
        attn_gain[0],
        attn_shift[0],
        mlp_gain[0],
        mlp_shift[0],
    )
    units = [vector.shape[0] // rows for vector in vectors]
    qkv_blocks = column_blocks(qkv_weight[0], width)
    small = pack_vectors([vector[None] for vector in vectors], 1, width)[0]
    attn_low = jnp.concatenate([qkv_blocks[: 2 * rows], small], axis=0)
    attn_high = jnp.concatenate(
        [qkv_blocks[2 * rows :], out_weight[0], jnp.zeros_like(small)], axis=0
    )
    mlp_low = column_blocks(up_weight[0], width)
    mlp_high = down_weight[0]
    pieces = []
    for low, high in ((attn_low, attn_high), (mlp_low, mlp_high)):
        arrived = swap(jnp.where(core == 0, high, low))
        own = jnp.where(core == 0, low, high)
        pieces.append((jnp.where(core == 0, own, arrived), jnp.where(core == 0, arrived, own)))
    gathered = [
        tuple(gather_dp(piece[layer], count) for piece in pieces)
        for layer in range(2)
    ]
    parameters = [unpack(gathered[layer], core, width, units) for layer in range(2)]

    seq_lengths = lax.dynamic_index_in_dim(lengths, core, 0, keepdims=False)[0]
    entry = lax.dynamic_index_in_dim(tokens, core, 0, keepdims=False).astype(jnp.float32)
    entries, keeps, results = ([], [], [])
    for layer in range(2):
        result, kept = layer_forward(entry, seq_lengths, parameters[layer])
        rounded = result.astype(jnp.bfloat16)
        entries.append(entry)
        keeps.append(kept)
        results.append(rounded)
        entry = rounded.astype(jnp.float32)

    def by_layer(first, second):
        own = jnp.where(core == 0, first, second)
        arrived = swap(jnp.where(core == 0, second, first))
        return jnp.stack(
            [jnp.where(core == 0, own, arrived), jnp.where(core == 0, arrived, own)]
        )

    layer_outputs = by_layer(*results)
    upstream = lax.dynamic_index_in_dim(cotangent, core, 0, keepdims=False).astype(jnp.float32)
    backs, mlps, attns = ([None, None], [None, None], [None, None])
    for layer in (1, 0):
        d_entry, grads = layer_backward(upstream, entries[layer], keeps[layer], parameters[layer])
        backs[layer] = d_entry
        upstream = d_entry.astype(jnp.bfloat16)
        if layer:
            upstream, totals = lax.optimization_barrier(
                (upstream, (pair_total(*mlp_pair(grads, count, width), core),
                            pair_total(*attn_pair(grads, count, width), core)))
            )
        else:
            totals = (pair_total(*mlp_pair(grads, count, width), core),
                      pair_total(*attn_pair(grads, count, width), core))
        mlps[layer], attns[layer] = (scatter_sum_dp(total, count) for total in totals)
        upstream = upstream.astype(jnp.float32)
    input_grads = by_layer(*backs)
    mlp_low, mlp_high = by_layer(*mlps).astype(jnp.float32)
    attn_low, attn_high = by_layer(*attns).astype(jnp.float32)
    grad_qkv = jnp.concatenate(
        [attn_low[:rows], attn_low[rows : 2 * rows], attn_high[:rows]], axis=1
    )
    grad_out = attn_high[rows : 2 * rows]
    grad_up = jnp.concatenate(jnp.split(mlp_low, mlp_low.shape[0] // rows, axis=0), axis=1)
    flat = attn_low[2 * rows :].reshape(-1)
    reduced, at = [grad_qkv, grad_out, grad_up, mlp_high], 0
    for size in units:
        reduced.append(flat[at : at + size * rows])
        at += size * rows
    return (layer_outputs[None], input_grads[None]) + tuple((piece[None] for piece in reduced))


def solution(mesh):
    placed = (
        P(None, "dp", None),
        P(None, "dp", None),
        P(None, "dp", None),
        P("section", "dp", None),
        P("section", "dp", None),
        P("section", "dp", None),
        P("section", "dp", None),
        P("section", "dp"),
        P("section", "dp"),
        P("section", "dp"),
        P("section", "dp"),
        P("section", "dp"),
        P("section", "dp"),
        P("section", "dp"),
        P("section", "dp"),
    )
    return jax.shard_map(
        on_device,
        mesh=mesh,
        in_specs=placed,
        out_specs=(
            P("section", None, "dp", None),
            P("section", None, "dp", None),
            P("section", "dp", None),
            P("section", "dp", None),
            P("section", "dp", None),
            P("section", "dp", None),
            P("section", "dp"),
            P("section", "dp"),
            P("section", "dp"),
            P("section", "dp"),
            P("section", "dp"),
            P("section", "dp"),
            P("section", "dp"),
            P("section", "dp"),
        ),
        check_vma=False,
    )
```
